128 devices in a mesh: branch: 8 (over z, y_lo), fsdp: 16 (over y_hi, x, core).
Axes of the slice: x: 4, y: 4 (y_hi: 2, y_lo: 2; y = y_hi * 2 + y_lo), z: 4, core: 2. Of those that a mesh axis runs over, the one named last changes fastest.
Arguments:
- tokens: bfloat16 [16384, 2048], P(('branch', 'fsdp')), may hold values from -6 to 6
- routes: int32 [16384, 2], P(('branch', 'fsdp')), may hold values from 0 to 7, all different within a row; in each aligned block of 128 rows (0 to 127, 128 to 255, ...) at most 34 rows name the same one
- gate_logits: float32 [16384, 8], P(('branch', 'fsdp')), may hold values from -8 to 8
- key_proj: bfloat16 [8, 2048, 1024], P('branch', 'fsdp'), may hold values from -6 to 6
- w_gate: bfloat16 [8, 2048, 8192], P('branch', 'fsdp'), may hold values from -0.125 to 0.125
- w_up: bfloat16 [8, 2048, 8192], P('branch', 'fsdp'), may hold values from -0.125 to 0.125
- w_down: bfloat16 [8, 8192, 2048], P('branch', 'fsdp'), may hold values from -0.0625 to 0.0625
Outputs:
- mixed: bfloat16 [16384, 2048], P(('branch', 'fsdp'))
- merged_keys: bfloat16 [2048, 1024], P('fsdp', 'branch')
The draws below stay inside these ranges and needn't reach their ends.
Inputs may be any that keep to these rules, and one draw needn't show every extreme that they name: `routes`: each row names two different experts. In each aligned block of 128 rows (the rows of one device) no expert is named by more than 34 rows, a bound that some block reaches.
All inputs are finite; a program needn't handle non-finite values.
Results may differ from the reference program's by a relative error of at most 0.02.
Values may be sent and summed in bfloat16 or wider, within the bound.
No kernel may reach another device: no remote copies, remote signals or barrier semaphores. Data moves between devices by JAX's collectives and lax.ppermute only.
A program may use at most 192 MiB of HBM per device.

```python
import math
import jax
import jax.numpy as jnp
import numpy as np
from jax import lax

D = 2048
FF = 8192
KVW = 1024
TOK_DEV = 128
NB = 8
CAP = 34
TOKENS = 16384
N_BRANCH = 8
N_FSDP = 16


def steps_of(rng, shape, pieces, smallest, largest):
    factor_of = 1.0
    for dim, blocks in pieces:
        steps = jax.random.uniform(jax.random.fold_in(jax.random.fold_in(rng, 6), dim), (blocks,), jnp.float32, smallest / len(pieces), largest / len(pieces))
        factor_of = factor_of * jnp.repeat(jnp.exp(steps), shape[dim] // blocks).reshape((-1,) + (1,) * (len(shape) - 1 - dim))
    return factor_of


def shared_out(own_key, own, number, rows, number_of, top, limit, slope):
    sequence = jax.random.permutation(own_key, number_of)
    heavy_load, usual = portions_of(number_of, rows * top, limit, slope, True), portions_of(number_of, rows * top, limit, slope, False)
    places = jnp.arange(number_of)

    def named(sizes, rotation):
        used = int((sizes > 0).sum())
        fixed = max(1, used // 4)
        shifted = fixed + (places - fixed + rotation * (used - fixed)) % max(1, number_of - fixed)
        return jnp.zeros((number_of,), jnp.int32).at[sequence[jnp.where(places < fixed, places, shifted)]].set(jnp.asarray(sizes, jnp.int32))

    sizes = jnp.where(number % 4 == 0, named(heavy_load, number // 4), named(usual, number - number // 4 - 1))
    mixed = jax.random.permutation(jax.random.fold_in(own, 3), number_of)
    donor, receiver = mixed[0:number_of // 2 * 2:2], mixed[1:number_of // 2 * 2:2]
    room = jnp.minimum(sizes[donor] - 1, limit - sizes[receiver]) // 2
    room = jnp.where((donor == sequence[0]) | (receiver == sequence[0]) | (sizes[receiver] == 0), 0, jnp.maximum(room, 0))
    shifted = jax.random.randint(jax.random.fold_in(own, 4), (number_of // 2,), 0, 1 << 20) % (room + 1)
    sizes = sizes.at[donor].add(-shifted).at[receiver].add(shifted)
    members = jnp.searchsorted(jnp.cumsum(sizes), jnp.arange(rows * top), side="right").astype(jnp.int32)
    grid = members.reshape(top, rows).T
    grid = grid[jax.random.permutation(jax.random.fold_in(own, 1), rows)]
    rotation = jax.random.randint(jax.random.fold_in(own, 2), (rows, 1), 0, top)
    return jnp.take_along_axis(grid, (jnp.arange(top)[None, :] + rotation) % top, axis=1)


def portions_of(amount, total, limit, lean, full):
    portions = [(1 << 20) // math.isqrt(standing ** lean) + 1 for standing in range(1, amount + 1)]
    largest = limit if full else min(limit, max(-(-total // amount), total * portions[0] // sum(portions)))
    least = 1 if total - largest >= amount - 1 else 0
    holding, rest = [largest] + [least] * (amount - 1), total - largest - least * (amount - 1)
    while rest > 0:
        free = [i for i in range(1, amount) if holding[i] < largest] or [i for i in range(1, amount) if holding[i] < limit]
        mass, remaining = sum([portions[i] for i in free]), rest
        for i in free:
            addition = min(limit - holding[i], max(1, remaining * portions[i] // mass), rest)
            holding[i] = holding[i] + addition
            rest = rest - addition
    return np.array(holding)


def scatter_about(own_key, dims, deviation, most, cuts=(), kind=jnp.bfloat16):
    entries = deviation * jax.random.normal(own_key, dims, jnp.float32)
    if cuts:
        entries = entries * steps_of(own_key, dims, cuts, -0.22, 0.18)
    return jnp.clip(entries, -most, most).astype(kind)


def setup_inputs(seed: int = 0) -> dict:
    key_list = jax.random.split(jax.random.key(seed), 8)
    tokens = scatter_about(key_list[0], (TOKENS, D), 1.0, 6.0, ((0, 128),))
    routes_keys = jax.random.split(jax.random.fold_in(key_list[1], 1), TOKENS // TOK_DEV)
    routes_turns = jax.random.permutation(jax.random.fold_in(key_list[1], 3), TOKENS // TOK_DEV)
    routes = jax.vmap(lambda own, number: shared_out(jax.random.fold_in(key_list[1], 2), own, number, TOK_DEV, NB, 2, CAP, 1))(routes_keys, routes_turns).reshape((TOKENS, 2))
    gate_logits = scatter_about(key_list[2], (TOKENS, NB), 2.0, 8.0, ((0, 128),), jnp.float32)
    key_proj = scatter_about(key_list[3], (NB, D, KVW), 1.0, 6.0, ((0, 8), (1, 16)))
    w_gate = scatter_about(key_list[4], (NB, D, FF), D ** -0.5, 0.125, ((0, 8), (1, 16)))
    w_up = scatter_about(key_list[5], (NB, D, FF), D ** -0.5, 0.125, ((0, 8), (1, 16)))
    w_down = scatter_about(key_list[6], (NB, FF, D), FF ** -0.5, 0.0625, ((0, 8), (1, 16)))
    return dict(tokens=tokens, routes=routes, gate_logits=gate_logits, key_proj=key_proj, w_gate=w_gate, w_up=w_up, w_down=w_down)


def place_slots(route_ids, experts, capacity):
    flat_ids = route_ids.reshape(-1).astype(jnp.int32)
    chosen = (flat_ids[:, None] == jnp.arange(experts, dtype=jnp.int32)[None, :]).astype(jnp.int32)
    earlier = jnp.cumsum(chosen, axis=0) - chosen
    position = jnp.sum(earlier * chosen, axis=1)
    return (flat_ids * capacity + position).astype(jnp.int32)


def fill_slots(token_rows, slot_ids, experts, capacity):
    count_rows = token_rows.shape[0]
    targets = jnp.arange(experts * capacity, dtype=jnp.int32)
    picker = jnp.sum((slot_ids.reshape(count_rows, 2)[None, :, :] == targets[:, None, None]).astype(jnp.int32), axis=2)
    placed = jnp.dot(picker.astype(jnp.bfloat16), token_rows, preferred_element_type=jnp.float32)
    return placed.astype(jnp.bfloat16)


def combine_rows(results, slot_ids, logit_rows, route_ids):
    experts = logit_rows.shape[1]
    chosen = route_ids[:, :, None] == jnp.arange(experts, dtype=jnp.int32)[None, None, :]
    picked = jnp.sum(jnp.where(chosen, logit_rows[:, None, :], jnp.float32(0.0)), axis=2)
    weights = jax.nn.sigmoid(picked - picked[:, ::-1])
    gathered = jnp.take(results, slot_ids, axis=0).reshape(route_ids.shape[0], 2, results.shape[1])
    return jnp.sum(gathered * weights[:, :, None], axis=1).astype(jnp.bfloat16)


def reference(tokens, routes, gate_logits, key_proj, w_gate, w_up, w_down):
    devices_all = N_BRANCH * N_FSDP
    merged_keys = (jnp.sum(key_proj.astype(jnp.float32), axis=0) / NB).astype(jnp.bfloat16)
    token_blocks = tokens.reshape(devices_all, TOK_DEV, D)
    route_blocks = routes.reshape(devices_all, TOK_DEV, 2)
    slot_ids = jax.vmap(lambda route_ids: place_slots(route_ids, NB, CAP))(route_blocks)
    dispatched = jax.vmap(lambda token_rows, slot_row: fill_slots(token_rows, slot_row, NB, CAP))(token_blocks, slot_ids)
    by_expert = dispatched.reshape(devices_all, NB, CAP, D).transpose(1, 0, 2, 3).reshape(NB, devices_all * CAP, D)
    shard_width = FF // N_FSDP

    def expert_output(operands):
        expert_rows, gate_matrix, up_matrix, down_matrix = operands
        gate_part = jnp.dot(expert_rows, gate_matrix, preferred_element_type=jnp.float32)
        up_part = jnp.dot(expert_rows, up_matrix, preferred_element_type=jnp.float32)
        hidden = (jax.nn.silu(gate_part) * up_part).astype(jnp.bfloat16)

        def add_shard(total, shard_index):
            hidden_part = lax.dynamic_slice_in_dim(hidden, shard_index * shard_width, shard_width, 1)
            down_part = lax.dynamic_slice_in_dim(down_matrix, shard_index * shard_width, shard_width, 0)
            partial_value = jnp.dot(hidden_part, down_part, preferred_element_type=jnp.float32).astype(jnp.bfloat16)
            partial_value = lax.optimization_barrier(partial_value)
            return total + partial_value.astype(jnp.float32), None

        total, _ = lax.scan(add_shard, jnp.zeros((expert_rows.shape[0], D), jnp.float32), jnp.arange(N_FSDP, dtype=jnp.int32))
        return total

    outputs = lax.map(expert_output, (by_expert, w_gate, w_up, w_down))
    per_device = outputs.reshape(NB, devices_all, CAP, D).transpose(1, 0, 2, 3).reshape(devices_all, NB * CAP, D)
    mixed = jax.vmap(combine_rows)(per_device, slot_ids, gate_logits.reshape(devices_all, TOK_DEV, NB), route_blocks)
    return (mixed.reshape(TOKENS, D), merged_keys)
```

```python
import functools

import jax
import jax.numpy as jnp
from jax import lax
from jax.experimental import pallas as pl
from jax.experimental.pallas import tpu as pltpu
from jax.sharding import PartitionSpec as P

BF = jnp.bfloat16
F32 = jnp.float32
NB = 8
CAP = 34
PAD = 48
KEY_AT = 40
TOK = 128
D = 2048
HALF = 1024
ROWS = NB * CAP
UNITS = 1024
REL_B = [(dz, dl) for dz in range(4) for dl in range(2)]
REL_F = [(dy, dx) for dy in range(2) for dx in range(4)]
VMEM = pl.BlockSpec(memory_space=pltpu.VMEM)
SMEM = pl.BlockSpec(memory_space=pltpu.SMEM)
ANY = pl.BlockSpec(memory_space=pl.ANY)


def perm_f(dy, dx, dc):
    return [
        (y * 8 + x * 2 + c, (y + dy) % 2 * 8 + (x + dx) % 4 * 2 + (c + dc) % 2)
        for y in range(2)
        for x in range(4)
        for c in range(2)
    ]


def perm_b(dz, dl):
    return [
        (z * 2 + w, (z + dz) % 4 * 2 + (w + dl) % 2) for z in range(4) for w in range(2)
    ]


def to_right(v):
    return lax.ppermute(v, "fsdp", perm_f(0, 1, 0))


def to_left(v):
    return lax.ppermute(v, "fsdp", perm_f(0, 3, 0))


def to_x(v, dx):
    return lax.ppermute(v, "fsdp", perm_f(0, dx, 0))


def to_y(v):
    return lax.ppermute(v, "fsdp", perm_f(1, 0, 0))


def to_core(v):
    return lax.ppermute(v, "fsdp", perm_f(0, 0, 1))


def iota(shape, dim):
    return lax.broadcasted_iota(jnp.int32, shape, dim)


def positions(routes_ref):
    lane = iota((TOK, 128), 1)
    chosen = (routes_ref[:, 0:1] == lane) | (routes_ref[:, 1:2] == lane)
    earlier = (iota((TOK, TOK), 1) < iota((TOK, TOK), 0)).astype(F32).astype(BF)
    count = jnp.dot(earlier, chosen.astype(F32).astype(BF), preferred_element_type=F32)
    return jnp.where(chosen, count, -1.0)


def dispatch_kernel(experts, routes, tokens, keys, *outs):
    by_expert = positions(routes).T
    sub = iota((128, TOK), 0)
    for r, out in enumerate(outs):
        e = experts[r]
        place = jnp.sum(jnp.where(sub == e, by_expert, 0.0), axis=0, keepdims=True)
        pick = (place == iota((KEY_AT, TOK), 0).astype(F32)).astype(F32).astype(BF)
        rows = jnp.dot(pick, tokens[...], preferred_element_type=F32)
        key = keys[:, pl.ds(pl.multiple_of(e * 128, 128), 128)].astype(F32)
        strip = jnp.concatenate([key[8 * m : 8 * m + 8] for m in range(16)], axis=1)
        out[...] = jnp.concatenate([rows, strip], axis=0).astype(BF)


def slot_matrix(rows_dim, shape):
    compact, padded = iota(shape, rows_dim), iota(shape, 1 - rows_dim)
    block = sum((padded >= PAD * m).astype(jnp.int32) for m in range(1, NB))
    j = padded - PAD * block
    return ((j < CAP) & (compact == block * CAP + j)).astype(F32).astype(BF)


def compact_kernel(*refs):
    msgs, (left, right, merged) = refs[:NB], refs[NB:]
    stacked = jnp.concatenate([m[...] for m in msgs], axis=0)
    rows = jnp.dot(slot_matrix(0, (ROWS, NB * PAD)), stacked, preferred_element_type=F32).astype(BF)
    left[...] = rows[:, :HALF]
    right[...] = rows[:, HALF:]
    total = functools.reduce(lambda a, b: a + b, [m[...].astype(F32)[KEY_AT:] for m in msgs])
    key = jnp.concatenate([total[:, 128 * m : 128 * m + 128] for m in range(16)], axis=0)
    merged[...] = (key / NB).astype(BF)


def pack_kernel(cols, gate, up, *refs):
    outs, sems = refs[:8], refs[8]
    copies = []
    for r, out in enumerate(outs):
        at = pl.ds(pl.multiple_of(cols[r] * UNITS, UNITS), UNITS)
        copies.append(pltpu.make_async_copy(gate.at[:, at], out.at[0], sems.at[2 * r]))
        copies.append(pltpu.make_async_copy(up.at[:, at], out.at[1], sems.at[2 * r + 1]))
    for copy in copies:
        copy.start()
    for copy in copies:
        copy.wait()


def ffn_kernel(widths, places, *refs):
    nx = sum(len(w) for w in widths)
    xs, refs = refs[:nx], refs[nx:]
    blocks, refs = refs[:16], refs[16:]
    downs, refs = refs[:2], refs[2:]
    outs, refs = refs[:8], refs[8:]
    rows, gate, up, down, hidden, sems = refs
    first, last = [], []
    at = 0
    for i, block in enumerate(widths):
        col = 0
        for w in block:
            dst = rows.at[pl.ds(i * ROWS, ROWS), pl.ds(col, w)]
            first.append(pltpu.make_async_copy(xs[at], dst, sems.at[at]))
            at, col = at + 1, col + w
    for r, block in enumerate(blocks):
        dst = pl.ds(pl.multiple_of(places[r] * 128, 128), 128)
        first.append(pltpu.make_async_copy(block.at[0], gate.at[dst, :], sems.at[at]))
        first.append(pltpu.make_async_copy(block.at[1], up.at[dst, :], sems.at[at + 1]))
        at += 2
    for r, block in enumerate(downs):
        dst = pl.ds(pl.multiple_of(places[16 + r] * 512, 512), 512)
        last.append(pltpu.make_async_copy(block, down.at[dst, :], sems.at[at]))
        at += 1
    for copy in first + last:
        copy.start()
    for copy in first:
        copy.wait()

    @pl.loop(0, UNITS // 256)
    def _(n):
        cols = pl.ds(pl.multiple_of(n * 256, 256), 256)
        for m in range(2):
            part = pl.ds(m * 2 * ROWS, 2 * ROWS)
            x = rows[part, :]
            g = jnp.dot(x, gate[:, cols], preferred_element_type=F32)
            u = jnp.dot(x, up[:, cols], preferred_element_type=F32)
            hidden[part, cols] = (g * (1.0 / (1.0 + jnp.exp(-g))) * u).astype(BF)

    for copy in last:
        copy.wait()
    for i in range(4):
        h = hidden[pl.ds(i * ROWS, ROWS), :]
        for k in range(2):
            for q in range(2):
                cols = pl.ds(k * HALF + q * 512, 512)
                y = jnp.dot(h, down[:, cols], preferred_element_type=F32)
                outs[2 * i + k][:, pl.ds(q * 512, 512)] = y.astype(BF)


def final_kernel(*refs):
    parts, outs = refs[:8], refs[8:]
    total = []
    for k in range(2):
        addends = [p[...].astype(F32) for p in parts[4 * k : 4 * k + 4]]
        total.append(functools.reduce(lambda a, b: a + b, addends).astype(BF))
    rows = jnp.concatenate(total, axis=1)
    spread = slot_matrix(1, (NB * PAD, ROWS))
    for r, out in enumerate(outs):
        out[...] = jnp.dot(
            spread[r * PAD : (r + 1) * PAD], rows, preferred_element_type=F32
        ).astype(BF)


def combine_kernel(experts, routes, logits, *refs):
    msgs, out = refs[:NB], refs[NB]
    place = positions(routes)
    lane = iota((TOK, 128), 1)
    wide = iota((1, NB * PAD), 1)
    block = sum((wide >= PAD * m).astype(jnp.int32) for m in range(1, NB))
    slot = (wide - PAD * block).astype(F32)
    owner = sum(jnp.where(block == r, experts[r], 0) for r in range(NB))
    stacked = jnp.concatenate([m[...] for m in msgs], axis=0)
    gathered, score = [], []
    for k in range(2):
        route = routes[:, k : k + 1]
        mine = jnp.sum(jnp.where(lane == route, place, 0.0), axis=1, keepdims=True)
        pick = ((owner == route) & (slot == mine)).astype(F32).astype(BF)
        gathered.append(jnp.dot(pick, stacked, preferred_element_type=F32))
        lane8 = iota((TOK, NB), 1)
        score.append(jnp.sum(jnp.where(lane8 == route, logits[...], 0.0), axis=1, keepdims=True))
    diff = score[0] - score[1]
    w0 = 1.0 / (1.0 + jnp.exp(-diff))
    w1 = 1.0 / (1.0 + jnp.exp(diff))
    out[...] = (gathered[0] * w0 + gathered[1] * w1).astype(BF)


def cost(flops, nbytes, trans=0):
    return pl.CostEstimate(flops=flops, bytes_accessed=nbytes, transcendentals=trans)


def params(mib):
    return pltpu.CompilerParams(vmem_limit_bytes=mib * 2**20)


def struct(*shape):
    return jax.ShapeDtypeStruct(shape, BF)


def feed_forward(xs, places, blocks, downs, name):
    widths = tuple(tuple(v.shape[1] for v in block) for block in xs)
    flat = [v for block in xs for v in block]
    return pl.pallas_call(
        functools.partial(ffn_kernel, widths),
        out_shape=[struct(ROWS, HALF)] * 8,
        in_specs=[SMEM] + [ANY] * (len(flat) + 18),
        out_specs=[VMEM] * 8,
        scratch_shapes=[
            pltpu.VMEM((4 * ROWS, D), BF),
            pltpu.VMEM((D, UNITS), BF),
            pltpu.VMEM((D, UNITS), BF),
            pltpu.VMEM((UNITS, D), BF),
            pltpu.VMEM((4 * ROWS, UNITS), BF),
            pltpu.SemaphoreType.DMA((len(flat) + 34,)),
        ],
        compiler_params=params(44),
        cost_estimate=cost(6 * 4 * ROWS * D * UNITS, 22_000_000, 4 * ROWS * UNITS),
        name=name,
    )(places, *flat, *blocks, *downs)


def add(a, b):
    return (a.astype(F32) + b.astype(F32)).astype(BF)


def per_device(tokens, routes, gate_logits, key_proj, w_gate, w_up, w_down):
    f = lax.axis_index("fsdp")
    b = lax.axis_index("branch")
    y, x, c = f // 8, f // 2 % 4, f % 2
    z, w = b // 2, b % 2
    experts = jnp.stack([(z + dz) % 4 * 2 + (w + dl) % 2 for dz, dl in REL_B]).astype(jnp.int32)
    columns = jnp.stack([(y + dy) % 2 * 4 + (x + dx) % 4 for dy, dx in REL_F]).astype(jnp.int32)
    origins = [((y - dy) % 2 * 4 + (x - dx) % 4) * 2 for dy, dx in REL_F]
    places = jnp.stack([o + c for o in origins] + [o + 1 - c for o in origins] + [c, 1 - c])
    places = places.astype(jnp.int32)

    sends = pl.pallas_call(
        dispatch_kernel,
        out_shape=[struct(PAD, D)] * NB,
        in_specs=[SMEM, VMEM, VMEM, VMEM],
        out_specs=[VMEM] * NB,
        compiler_params=params(32),
        cost_estimate=cost(2 * NB * PAD * TOK * D, 2_500_000),
        name="dispatch",
    )(experts, routes, tokens, key_proj[0])
    msgs = [sends[0]] + [
        lax.ppermute(sends[r], "branch", perm_b(*REL_B[r])) for r in range(1, NB)
    ]

    packed = pl.pallas_call(
        pack_kernel,
        out_shape=[struct(2, 128, UNITS)] * 8,
        in_specs=[SMEM, ANY, ANY],
        out_specs=[ANY] * 8,
        scratch_shapes=[pltpu.SemaphoreType.DMA((16,))],
        cost_estimate=cost(0, 16_000_000),
        name="pack",
    )(columns, w_gate[0], w_up[0])
    mine = {0: packed[0]}
    for dx in (2, 1, 3):
        mine[dx] = to_x(packed[dx], dx)
    other = {}
    for dx in (2, 1, 3, 0):
        came = to_y(packed[4 + dx])
        other[dx] = to_x(came, dx) if dx else came
    blocks = [mine[dx] for dx in range(4)] + [other[dx] for dx in range(4)]
    blocks = blocks + [to_core(v) for v in blocks]
    downs = [w_down[0], to_core(w_down[0])]

    own_a, own_b, merged_keys = pl.pallas_call(
        compact_kernel,
        out_shape=[struct(ROWS, HALF), struct(ROWS, HALF), struct(128, 128)],
        in_specs=[VMEM] * NB,
        out_specs=[VMEM] * 3,
        compiler_params=params(32),
        cost_estimate=cost(2 * ROWS * NB * PAD * D, 2_700_000),
        name="compact",
    )(*msgs)

    left_a, right_a = to_right(own_a), to_left(own_a)
    left_b, right_b = to_right(own_b), to_left(own_b)
    far_a, far_b = to_right(left_a), to_left(right_b)
    p_own_a = to_y(own_a)
    p_left_a, p_right_a = to_right(p_own_a), to_left(p_own_a)
    p_far_0, p_far_1 = to_right(p_left_a[:, :512]), to_left(p_right_a[:, 512:])
    p_own_b, p_left_b, p_right_b, p_far_b = (to_y(v) for v in (own_b, left_b, right_b, far_b))

    here = feed_forward(
        [(far_a, far_b), (left_a, left_b), (right_a, right_b), (own_a, own_b)],
        places, blocks, downs, "ffn_here",
    )
    there = feed_forward(
        [
            (p_far_0, p_far_1, p_far_b),
            (p_left_a, p_left_b),
            (p_right_a, p_right_b),
            (p_own_a, p_own_b),
        ],
        places, blocks, downs, "ffn_there",
    )
    far_a, far_b, left_a, left_b, right_a, right_b, own_a, own_b = here
    q_far_a, q_far_b, q_left_a, q_left_b, q_right_a, q_right_b, q_own_a, q_own_b = there

    passing = to_right(far_a)
    got_0 = to_left(left_a)
    got_1 = to_right(add(right_a, passing))
    passing = to_left(q_far_a)
    got_2 = to_right(q_right_a)
    got_3 = to_left(add(q_left_a, passing))
    swapped = to_y(
        (q_own_a.astype(F32) + got_2.astype(F32) + got_3.astype(F32)).astype(BF)
    )
    far_b = add(far_b, to_y(q_far_b))
    right_b = add(right_b, to_y(q_right_b))
    left_b = add(left_b, to_y(q_left_b))
    own_q = to_y(q_own_b)
    passing = to_left(far_b)
    got_4 = to_right(right_b)
    got_5 = to_left(add(left_b, passing))

    returns = pl.pallas_call(
        final_kernel,
        out_shape=[struct(PAD, D)] * NB,
        in_specs=[VMEM] * 8,
        out_specs=[VMEM] * NB,
        compiler_params=params(32),
        cost_estimate=cost(2 * NB * PAD * ROWS * D, 6_000_000),
        name="spread",
    )(own_a, got_0, got_1, swapped, own_b, own_q, got_4, got_5)
    results = [returns[0]] + [
        lax.ppermute(returns[r], "branch", perm_b(-REL_B[r][0], -REL_B[r][1]))
        for r in range(1, NB)
    ]
    mixed = pl.pallas_call(
        combine_kernel,
        out_shape=struct(TOK, D),
        in_specs=[SMEM, VMEM, VMEM] + [VMEM] * NB,
        out_specs=VMEM,
        compiler_params=params(32),
        cost_estimate=cost(4 * NB * PAD * TOK * D, 2_200_000),
        name="combine",
    )(experts, routes, gate_logits, *results)
    return mixed, merged_keys


def solution(mesh):
    placed = (
        P(("branch", "fsdp"), None),
        P(("branch", "fsdp"), None),
        P(("branch", "fsdp"), None),
        P("branch", "fsdp", None),
        P("branch", "fsdp", None),
        P("branch", "fsdp", None),
        P("branch", "fsdp", None),
    )
    return jax.shard_map(
        per_device,
        mesh=mesh,
        in_specs=placed,
        out_specs=(P(("branch", "fsdp"), None), P("fsdp", "branch")),
        check_vma=False,
    )
```

```python
import functools

import jax
import jax.numpy as jnp
from jax import lax
from jax.experimental import pallas as pl
from jax.experimental.pallas import tpu as pltpu
from jax.sharding import PartitionSpec as P

BF = jnp.bfloat16
F32 = jnp.float32
NB = 8
CAP = 34
PAD = 48
BACK = 40
KEY_AT = 40
TOK = 128
D = 2048
SPLIT = 1280
ROWS = NB * CAP
UNITS = 1024
REL_B = [(dz, dl) for dz in range(4) for dl in range(2)]
VMEM = pl.BlockSpec(memory_space=pltpu.VMEM)
HBM = pl.BlockSpec(memory_space=pltpu.HBM)
SMEM = pl.BlockSpec(memory_space=pltpu.SMEM)


def perm_f(dy, dx, dc):
    return [
        (y * 8 + x * 2 + c, (y + dy) % 2 * 8 + (x + dx) % 4 * 2 + (c + dc) % 2)
        for y in range(2)
        for x in range(4)
        for c in range(2)
    ]


RING = [
    (y * 8 + x * 2 + c, y * 8 + (x + 1 - 2 * c) % 4 * 2 + c)
    for y in range(2)
    for x in range(4)
    for c in range(2)
]


def perm_b(dz, dl):
    return [
        (z * 2 + w, (z + dz) % 4 * 2 + (w + dl) % 2) for z in range(4) for w in range(2)
    ]


def along(v):
    return lax.ppermute(v, "fsdp", RING)


def against(v):
    return lax.ppermute(v, "fsdp", [(d, s) for s, d in RING])


def to_y(v):
    return lax.ppermute(v, "fsdp", perm_f(1, 0, 0))


def to_chips(v):
    return lax.all_to_all(
        v, "fsdp", 0, 0, tiled=True,
        axis_index_groups=[[2 * k + c for k in range(8)] for c in range(2)],
    )


def to_core(v):
    return lax.ppermute(v, "fsdp", perm_f(0, 0, 1))


def iota(shape, dim):
    return lax.broadcasted_iota(jnp.int32, shape, dim)


def positions(routes_ref):
    lane = iota((TOK, 128), 1)
    chosen = (routes_ref[:, 0:1] == lane) | (routes_ref[:, 1:2] == lane)
    earlier = (iota((TOK, TOK), 1) < iota((TOK, TOK), 0)).astype(F32).astype(BF)
    count = jnp.dot(earlier, chosen.astype(F32).astype(BF), preferred_element_type=F32)
    return jnp.where(chosen, count, -1.0)


def dispatch_kernel(experts, routes, tokens, keys, *outs):
    by_expert = positions(routes).T
    sub = iota((128, TOK), 0)
    for r, out in enumerate(outs):
        e = experts[r]
        place = jnp.sum(jnp.where(sub == e, by_expert, 0.0), axis=0, keepdims=True)
        pick = (place == iota((KEY_AT, TOK), 0).astype(F32)).astype(F32).astype(BF)
        rows = jnp.dot(pick, tokens[...], preferred_element_type=F32)
        key = keys[:, pl.ds(pl.multiple_of(e * 128, 128), 128)].astype(F32)
        strip = jnp.concatenate([key[8 * m : 8 * m + 8] for m in range(16)], axis=1)
        out[...] = jnp.concatenate([rows, strip], axis=0).astype(BF)


def slot_matrix(rows_dim, shape, pad):
    compact, padded = iota(shape, rows_dim), iota(shape, 1 - rows_dim)
    block = sum((padded >= pad * m).astype(jnp.int32) for m in range(1, NB))
    j = padded - pad * block
    return ((j < CAP) & (compact == block * CAP + j)).astype(F32).astype(BF)


def compact_kernel(*refs):
    msgs, (out, merged) = refs[:NB], refs[NB:]
    stacked = jnp.concatenate([m[...] for m in msgs], axis=0)
    pick = slot_matrix(0, (ROWS, NB * PAD), PAD)
    out[...] = jnp.dot(pick, stacked, preferred_element_type=F32).astype(BF)
    total = functools.reduce(lambda a, b: a + b, [m[...].astype(F32)[KEY_AT:] for m in msgs])
    key = jnp.concatenate([total[:, 128 * m : 128 * m + 128] for m in range(16)], axis=0)
    merged[...] = (key / NB).astype(BF)


def pack_kernel(src, out):
    out[0] = src[...]


def pack(matrix, name):
    return pl.pallas_call(
        pack_kernel,
        grid=(8,),
        out_shape=struct(8, 128, UNITS),
        in_specs=[pl.BlockSpec((128, UNITS), lambda j: (0, j))],
        out_specs=pl.BlockSpec((1, 128, UNITS), lambda j: (j, 0, 0)),
        compiler_params=params(48),
        cost_estimate=cost(0, 8_000_000),
        name="pack_" + name,
    )(matrix)


def ffn_kernel(widths, core, *refs):
    nx = sum(len(w) for w in widths)
    xs, refs = refs[:nx], refs[nx:]
    sources, refs = refs[:6], refs[6:]
    outs, (rows, hidden, held, down, sems) = refs[:4], refs[4:]
    c = core[0]
    steps = []
    for n in range(4):
        cols = pl.ds(256 * n, 256)
        steps.append(
            [
                pltpu.make_async_copy(
                    src.at[:, :, cols], held.at[i, :, :, cols], sems.at[4 * n + i]
                )
                for i, src in enumerate(sources[:4])
            ]
        )
    last = [
        pltpu.make_async_copy(src, down.at[pl.ds(512 * i, 512), :], sems.at[16 + i])
        for i, src in enumerate(sources[4:])
    ]
    for copy in sum(steps, []) + last:
        copy.start()
    at = 0
    for i, block in enumerate(widths):
        col = 0
        for w in block:
            for k in range(w // 256):
                for side, place in enumerate((c, 1 - c)):
                    src = pl.ds(pl.multiple_of(256 * k + 128 * place, 128), 128)
                    dst = pl.ds(col + 256 * k + 128 * side, 128)
                    rows[pl.ds(i * ROWS, ROWS), dst] = xs[at][:, src]
            at, col = at + 1, col + w
    for n in range(4):
        for copy in steps[n]:
            copy.wait()
        cols = slice(256 * n, 256 * n + 256)
        x = rows[...]
        weights = [
            jnp.concatenate([held[2 * k + j, i, :, cols] for i in range(8) for j in range(2)], axis=0)
            for k in range(2)
        ]
        g = jnp.dot(x, weights[0], preferred_element_type=F32)
        u = jnp.dot(x, weights[1], preferred_element_type=F32)
        hidden[:, cols] = (g * (1.0 / (1.0 + jnp.exp(-g))) * u).astype(BF)
    for copy in last:
        copy.wait()
    h = jnp.concatenate(
        [hidden[:, pl.ds(pl.multiple_of(512 * p, 512), 512)] for p in (c, 1 - c)], axis=1
    )
    for at, end in ((0, SPLIT), (SPLIT, D)):
        for low in range(at, end, 512):
            high = min(low + 512, end)
            v = jnp.dot(h, down[:, low:high], preferred_element_type=F32).astype(BF)
            for i in range(2):
                outs[2 * i + (at > 0)][:, low - at : high - at] = v[i * ROWS : (i + 1) * ROWS]


def final_kernel(sources, *refs):
    parts, out = refs[:8], refs[8]
    total = []
    for k in range(2):
        addends = [p[...].astype(F32) for p in parts[4 * k : 4 * k + 4]]
        total.append(functools.reduce(lambda a, b: a + b, addends).astype(BF))
    rows = jnp.concatenate(total, axis=1)
    spread = slot_matrix(1, (NB * BACK, ROWS), BACK)
    wide = jnp.dot(spread, rows, preferred_element_type=F32)
    for r in range(NB):
        out[sources[r]] = wide[r * BACK : (r + 1) * BACK].astype(BF)


def combine_kernel(routes, logits, msgs, out):
    place = positions(routes)
    lane = iota((TOK, 128), 1)
    wide = iota((1, NB * BACK), 1)
    owner = sum((wide >= BACK * m).astype(jnp.int32) for m in range(1, NB))
    slot = (wide - BACK * owner).astype(F32)
    stacked = jnp.concatenate([msgs[r] for r in range(NB)], axis=0)
    gathered, score = [], []
    for k in range(2):
        route = routes[:, k : k + 1]
        mine = jnp.sum(jnp.where(lane == route, place, 0.0), axis=1, keepdims=True)
        pick = ((owner == route) & (slot == mine)).astype(F32).astype(BF)
        gathered.append(jnp.dot(pick, stacked, preferred_element_type=F32))
        lane8 = iota((TOK, NB), 1)
        score.append(jnp.sum(jnp.where(lane8 == route, logits[...], 0.0), axis=1, keepdims=True))
    diff = score[0] - score[1]
    w0 = 1.0 / (1.0 + jnp.exp(-diff))
    w1 = 1.0 / (1.0 + jnp.exp(diff))
    out[...] = (gathered[0] * w0 + gathered[1] * w1).astype(BF)


def cost(flops, nbytes, trans=0):
    return pl.CostEstimate(flops=flops, bytes_accessed=nbytes, transcendentals=trans)


def params(mib):
    return pltpu.CompilerParams(vmem_limit_bytes=mib * 2**20)


def struct(*shape):
    return jax.ShapeDtypeStruct(shape, BF)


def feed_forward(xs, core, weights, name):
    widths = tuple(tuple(v.shape[1] for v in block) for block in xs)
    flat = [v for block in xs for v in block]
    return pl.pallas_call(
        functools.partial(ffn_kernel, widths),
        out_shape=[struct(ROWS, SPLIT), struct(ROWS, D - SPLIT)] * 2,
        in_specs=[SMEM] + [VMEM] * len(flat) + [HBM] * 6,
        out_specs=[VMEM] * 4,
        scratch_shapes=[
            pltpu.VMEM((2 * ROWS, D), BF),
            pltpu.VMEM((2 * ROWS, UNITS), BF),
            pltpu.VMEM((4, 8, 128, UNITS), BF),
            pltpu.VMEM((UNITS, D), BF),
            pltpu.SemaphoreType.DMA((18,)),
        ],
        compiler_params=params(28),
        cost_estimate=cost(6 * 2 * ROWS * D * UNITS, 18_000_000, 2 * ROWS * UNITS),
        name=name,
    )(core, *flat, *weights)


def add(a, b):
    return (a.astype(F32) + b.astype(F32)).astype(BF)


def per_device(tokens, routes, gate_logits, key_proj, w_gate, w_up, w_down):
    f = lax.axis_index("fsdp")
    core = (f % 2).astype(jnp.int32).reshape(1)

    b = lax.axis_index("branch")
    experts = jnp.stack([(b // 2 + dz) % 4 * 2 + (b + dl) % 2 for dz, dl in REL_B])

    sends = pl.pallas_call(
        dispatch_kernel,
        out_shape=[struct(PAD, D)] * NB,
        grid=(1,),
        in_specs=[SMEM] + [pl.BlockSpec((TOK, n), lambda i: (0, 0)) for n in (2, D, 1024)],
        out_specs=[VMEM] * NB,
        compiler_params=params(12),
        cost_estimate=cost(2 * NB * PAD * TOK * D, 2_500_000),
        name="dispatch",
    )(experts.astype(jnp.int32), routes, tokens, key_proj[0])
    msgs = [sends[0]] + [
        lax.ppermute(sends[r], "branch", perm_b(*REL_B[r])) for r in range(1, NB)
    ]
    own, merged_keys = pl.pallas_call(
        compact_kernel,
        out_shape=[struct(ROWS, D), struct(128, 128)],
        in_specs=[VMEM] * NB,
        out_specs=[VMEM] * 2,
        compiler_params=params(12),
        cost_estimate=cost(2 * ROWS * NB * PAD * D, 2_700_000),
        name="compact",
    )(*msgs)

    down_other = to_core(w_down[0])
    gate, down_other = lax.optimization_barrier((pack(w_gate[0], "gate"), down_other))
    gate = to_chips(gate)
    up, own, gate = lax.optimization_barrier((pack(w_up[0], "up"), own, gate))
    up = to_chips(up)
    gate_other = to_core(gate)

    back, front, p_own = along(own), against(own), to_y(own)
    up, back, front, p_own, gate_other = lax.optimization_barrier(
        (up, back, front, p_own, gate_other)
    )
    far = along(back)
    p_own_a = p_own[:, :SPLIT]
    p_back_a, p_front_a = along(p_own_a), against(p_own_a)
    p_back_b, p_front_b, p_far_b = (to_y(v[:, SPLIT:]) for v in (back, front, far))
    weights = [gate, gate_other, up, to_core(up), w_down[0], down_other]

    front_a, front_b, own_a, own_b = feed_forward(
        [(front,), (own,)], core, weights, "ffn_here_1"
    )
    p_back_a, own_a = lax.optimization_barrier((p_back_a, own_a))
    p_far_a = along(p_back_a)
    far_a, far_b, back_a, back_b = feed_forward([(far,), (back,)], core, weights, "ffn_here_0")
    p_far_a, own_a, far_a = lax.optimization_barrier((p_far_a, own_a, far_a))
    q_far_a, q_far_b, q_back_a, q_back_b = feed_forward(
        [(p_far_a, p_far_b), (p_back_a, p_back_b)], core, weights, "ffn_there_0"
    )
    got_0, passing = against(back_a), along(far_a)
    p_front_a, got_0, passing = lax.optimization_barrier((p_front_a, got_0, passing))
    q_front_a, q_front_b, q_own_a, q_own_b = feed_forward(
        [(p_front_a, p_front_b), (p_own,)], core, weights, "ffn_there_1"
    )

    got_1 = along(add(front_a, passing))
    got_2 = against(q_back_a)
    got_3 = along(add(q_front_a, along(q_far_a)))
    swapped = to_y((q_own_a.astype(F32) + got_2.astype(F32) + got_3.astype(F32)).astype(BF))
    got_5 = along(add(add(front_b, to_y(q_front_b)), along(add(far_b, to_y(q_far_b)))))
    got_4 = against(add(back_b, to_y(q_back_b)))
    own_q = to_y(q_own_b)

    sources = jnp.stack([(b // 2 - dz) % 4 * 2 + (b - dl) % 2 for dz, dl in REL_B])
    returns = pl.pallas_call(
        final_kernel,
        out_shape=struct(NB, BACK, D),
        in_specs=[SMEM] + [VMEM] * 8,
        out_specs=VMEM,
        compiler_params=params(16),
        cost_estimate=cost(2 * NB * BACK * ROWS * D, 6_000_000),
        name="spread",
    )(sources.astype(jnp.int32), own_a, got_0, got_1, swapped, own_b, own_q, got_4, got_5)
    results = lax.all_to_all(returns, "branch", 0, 0, tiled=True)
    mixed = pl.pallas_call(
        combine_kernel,
        out_shape=struct(TOK, D),
        in_specs=[VMEM] * 3,
        out_specs=VMEM,
        compiler_params=params(12),
        cost_estimate=cost(4 * NB * BACK * TOK * D, 2_200_000),
        name="combine",
    )(routes, gate_logits, results)
    return mixed, merged_keys


def solution(mesh):
    placed = (
        P(("branch", "fsdp"), None),
        P(("branch", "fsdp"), None),
        P(("branch", "fsdp"), None),
        P("branch", "fsdp", None),
        P("branch", "fsdp", None),
        P("branch", "fsdp", None),
        P("branch", "fsdp", None),
    )
    return jax.shard_map(
        per_device,
        mesh=mesh,
        in_specs=placed,
        out_specs=(P(("branch", "fsdp"), None), P("fsdp", "branch")),
        check_vma=False,
    )
```

```python
import functools

import jax
import jax.numpy as jnp
from jax import lax
from jax.experimental import pallas as pl
from jax.experimental.pallas import tpu as pltpu
from jax.sharding import PartitionSpec as P

BF = jnp.bfloat16
F32 = jnp.float32
NB = 8
CAP = 34
PAD = 48
BACK = 40
KEY_AT = 40
TOK = 128
D = 2048
SPLIT_IN = 1536
SPLIT_OUT = 1280
ROWS = NB * CAP
UNITS = 1024
REL_B = [(dz, dl) for dz in range(4) for dl in range(2)]
VMEM = pl.BlockSpec(memory_space=pltpu.VMEM)
HBM = pl.BlockSpec(memory_space=pltpu.HBM)
SMEM = pl.BlockSpec(memory_space=pltpu.SMEM)


def perm_f(dy, dx, dc):
    return [
        (y * 8 + x * 2 + c, (y + dy) % 2 * 8 + (x + dx) % 4 * 2 + (c + dc) % 2)
        for y in range(2)
        for x in range(4)
        for c in range(2)
    ]


RING = [
    (y * 8 + x * 2 + c, y * 8 + (x + 1 - 2 * c) % 4 * 2 + c)
    for y in range(2)
    for x in range(4)
    for c in range(2)
]


def perm_b(dz, dl):
    return [
        (z * 2 + w, (z + dz) % 4 * 2 + (w + dl) % 2) for z in range(4) for w in range(2)
    ]


def along(v):
    return lax.ppermute(v, "fsdp", RING)


def against(v):
    return lax.ppermute(v, "fsdp", [(d, s) for s, d in RING])


def to_y(v):
    return lax.ppermute(v, "fsdp", perm_f(1, 0, 0))


def to_columns(v):
    return lax.all_to_all(
        v, "fsdp", 0, 0, tiled=True,
        axis_index_groups=[[8 * y + 2 * k + c for k in range(4)] for y in range(2) for c in range(2)],
    )


def to_core(v):
    return lax.ppermute(v, "fsdp", perm_f(0, 0, 1))


def iota(shape, dim):
    return lax.broadcasted_iota(jnp.int32, shape, dim)


def positions(routes_ref):
    lane = iota((TOK, 128), 1)
    chosen = (routes_ref[:, 0:1] == lane) | (routes_ref[:, 1:2] == lane)
    earlier = (iota((TOK, TOK), 1) < iota((TOK, TOK), 0)).astype(F32).astype(BF)
    count = jnp.dot(earlier, chosen.astype(F32).astype(BF), preferred_element_type=F32)
    return jnp.where(chosen, count, -1.0)


def dispatch_kernel(experts, routes, tokens, keys, *outs):
    by_expert = positions(routes).T
    sub = iota((128, TOK), 0)
    for r, out in enumerate(outs):
        e = experts[r]
        place = jnp.sum(jnp.where(sub == e, by_expert, 0.0), axis=0, keepdims=True)
        pick = (place == iota((KEY_AT, TOK), 0).astype(F32)).astype(F32).astype(BF)
        rows = jnp.dot(pick, tokens[...], preferred_element_type=F32)
        key = keys[:, pl.ds(pl.multiple_of(e * 128, 128), 128)].astype(F32)
        strip = jnp.concatenate([key[8 * m : 8 * m + 8] for m in range(16)], axis=1)
        out[...] = jnp.concatenate([rows, strip], axis=0).astype(BF)


def slot_matrix(rows_dim, shape, pad):
    compact, padded = iota(shape, rows_dim), iota(shape, 1 - rows_dim)
    block = sum((padded >= pad * m).astype(jnp.int32) for m in range(1, NB))
    j = padded - pad * block
    return ((j < CAP) & (compact == block * CAP + j)).astype(F32).astype(BF)


def compact_kernel(*refs):
    msgs, (out, merged) = refs[:NB], refs[NB:]
    stacked = jnp.concatenate([m[...] for m in msgs], axis=0)
    pick = slot_matrix(0, (ROWS, NB * PAD), PAD)
    out[...] = jnp.dot(pick, stacked, preferred_element_type=F32).astype(BF)
    total = functools.reduce(lambda a, b: a + b, [m[...].astype(F32)[KEY_AT:] for m in msgs])
    key = jnp.concatenate([total[:, 128 * m : 128 * m + 128] for m in range(16)], axis=0)
    merged[...] = (key / NB).astype(BF)


def pack_kernel(first, gate, up, out):
    out[0, 0] = gate[...]
    out[0, 1] = up[...]


def pack(first, gate, up, name):
    return pl.pallas_call(
        pack_kernel,
        grid_spec=pltpu.PrefetchScalarGridSpec(
            num_scalar_prefetch=1,
            grid=(4,),
            in_specs=[pl.BlockSpec((128, UNITS), lambda j, first: (0, first[0] + j))] * 2,
            out_specs=pl.BlockSpec((1, 2, 128, UNITS), lambda j, first: (j, 0, 0, 0)),
        ),
        out_shape=struct(4, 2, 128, UNITS),
        compiler_params=params(48),
        cost_estimate=cost(0, 8_000_000),
        name="pack_" + name,
    )(first, gate, up)


def ffn_kernel(widths, core, *refs):
    nx = sum(len(w) for w in widths)
    xs, refs = refs[:nx], refs[nx:]
    sources, refs = refs[:8], refs[8:]
    outs, (hidden, held, down, sems) = refs[:4], refs[4:]
    c, y = core[0], core[1]
    every, low, high = pl.ds(0, 4), pl.ds(0, 2), pl.ds(2, 2)
    places = ((y, c, every), (y, 1 - c, every))
    places += ((1 - y, c, low), (1 - y, 1 - c, low), (1 - y, c, high), (1 - y, 1 - c, high))
    steps = []
    for n in range(4):
        cols = pl.ds(256 * n, 256)
        steps.append(
            [
                pltpu.make_async_copy(
                    src.at[:, :, :, cols], held.at[(*places[i], slice(None), slice(None), cols)],
                    sems.at[6 * n + i],
                )
                for i, src in enumerate(sources[:6])
            ]
        )
    steps.append(
        [
            pltpu.make_async_copy(src, down.at[places[i][1]], sems.at[24 + i])
            for i, src in enumerate(sources[6:])
        ]
    )
    for copy in steps[0] + steps[1]:
        copy.start()
    at, blocks = 0, []
    for block in widths:
        pieces = [xs[at + i][...] for i in range(len(block))]
        blocks.append(jnp.concatenate(pieces, axis=1) if len(pieces) > 1 else pieces[0])
        at += len(block)
    x = jnp.concatenate(blocks, axis=0)
    for n in range(4):
        for copy in steps[n]:
            copy.wait()
        if n < 3:
            for copy in steps[n + 2]:
                copy.start()
        cols = slice(256 * n, 256 * n + 256)
        weights = [
            jnp.concatenate([held[i // 4, j, i % 4, k, :, cols] for i in range(8) for j in range(2)])
            for k in range(2)
        ]
        g = jnp.dot(x, weights[0], preferred_element_type=F32)
        u = jnp.dot(x, weights[1], preferred_element_type=F32)
        hidden[:, cols] = (g * (1.0 / (1.0 + jnp.exp(-g))) * u).astype(BF)
    for copy in steps[4]:
        copy.wait()
    h = hidden[...]
    for at, end in ((0, SPLIT_OUT), (SPLIT_OUT, D)):
        for low in range(at, end, 512):
            high = min(low + 512, end)
            w = jnp.concatenate([down[j, :, low:high] for j in range(2)], axis=0)
            v = jnp.dot(h, w, preferred_element_type=F32).astype(BF)
            for i in range(2):
                outs[2 * i + (at > 0)][:, low - at : high - at] = v[i * ROWS : (i + 1) * ROWS]


def final_kernel(sources, *refs):
    parts, out = refs[:8], refs[8]
    total = []
    for k in range(2):
        addends = [p[...].astype(F32) for p in parts[4 * k : 4 * k + 4]]
        total.append(functools.reduce(lambda a, b: a + b, addends).astype(BF))
    rows = jnp.concatenate(total, axis=1)
    spread = slot_matrix(1, (NB * BACK, ROWS), BACK)
    wide = jnp.dot(spread, rows, preferred_element_type=F32)
    for r in range(NB):
        out[sources[r]] = wide[r * BACK : (r + 1) * BACK].astype(BF)


def combine_kernel(routes, logits, msgs, out):
    place = positions(routes)
    lane = iota((TOK, 128), 1)
    wide = iota((1, NB * BACK), 1)
    owner = sum((wide >= BACK * m).astype(jnp.int32) for m in range(1, NB))
    slot = (wide - BACK * owner).astype(F32)
    stacked = jnp.concatenate([msgs[r] for r in range(NB)], axis=0)
    gathered, score = [], []
    for k in range(2):
        route = routes[:, k : k + 1]
        mine = jnp.sum(jnp.where(lane == route, place, 0.0), axis=1, keepdims=True)
        pick = ((owner == route) & (slot == mine)).astype(F32).astype(BF)
        gathered.append(jnp.dot(pick, stacked, preferred_element_type=F32))
        lane8 = iota((TOK, NB), 1)
        score.append(jnp.sum(jnp.where(lane8 == route, logits[...], 0.0), axis=1, keepdims=True))
    diff = score[0] - score[1]
    w0 = 1.0 / (1.0 + jnp.exp(-diff))
    w1 = 1.0 / (1.0 + jnp.exp(diff))
    out[...] = (gathered[0] * w0 + gathered[1] * w1).astype(BF)


def cost(flops, nbytes, trans=0):
    return pl.CostEstimate(flops=flops, bytes_accessed=nbytes, transcendentals=trans)


def params(mib):
    return pltpu.CompilerParams(vmem_limit_bytes=mib * 2**20)


def struct(*shape):
    return jax.ShapeDtypeStruct(shape, BF)


def feed_forward(xs, core, weights, name):
    widths = tuple(tuple(v.shape[1] for v in block) for block in xs)
    flat = [v for block in xs for v in block]
    return pl.pallas_call(
        functools.partial(ffn_kernel, widths),
        out_shape=[struct(ROWS, SPLIT_OUT), struct(ROWS, D - SPLIT_OUT)] * 2,
        in_specs=[SMEM] + [VMEM] * len(flat) + [HBM] * 8,
        out_specs=[VMEM] * 4,
        scratch_shapes=[
            pltpu.VMEM((2 * ROWS, UNITS), BF),
            pltpu.VMEM((2, 2, 4, 2, 128, UNITS), BF),
            pltpu.VMEM((2, 512, D), BF),
            pltpu.SemaphoreType.DMA((26,)),
        ],
        compiler_params=params(46),
        cost_estimate=cost(6 * 2 * ROWS * D * UNITS, 18_000_000, 2 * ROWS * UNITS),
        name=name,
    )(core, *flat, *weights)


def add(a, b):
    return (a.astype(F32) + b.astype(F32)).astype(BF)


def per_device(tokens, routes, gate_logits, key_proj, w_gate, w_up, w_down):
    f = lax.axis_index("fsdp")
    y = f // 8
    core = jnp.stack([f % 2, y]).astype(jnp.int32)

    b = lax.axis_index("branch")
    experts = jnp.stack([(b // 2 + dz) % 4 * 2 + (b + dl) % 2 for dz, dl in REL_B])

    sends = pl.pallas_call(
        dispatch_kernel,
        out_shape=[struct(PAD, D)] * NB,
        grid=(1,),
        in_specs=[SMEM] + [pl.BlockSpec((TOK, n), lambda i: (0, 0)) for n in (2, D, 1024)],
        out_specs=[VMEM] * NB,
        compiler_params=params(12),
        cost_estimate=cost(2 * NB * PAD * TOK * D, 2_500_000),
        name="dispatch",
    )(experts.astype(jnp.int32), routes, tokens, key_proj[0])
    msgs = [sends[0]] + [
        lax.ppermute(sends[r], "branch", perm_b(*REL_B[r])) for r in range(1, NB)
    ]
    down_other = to_core(w_down[0])
    first = jnp.stack([4 * y, 4 - 4 * y]).astype(jnp.int32)
    crossing = pack(first[1:], w_gate[0], w_up[0], "other")
    crossing, down_other = lax.optimization_barrier((crossing, down_other))
    crossing = to_columns(crossing)
    staying = pack(first[:1], w_gate[0], w_up[0], "own")
    staying, crossing, msgs[1:6] = lax.optimization_barrier((staying, crossing, msgs[1:6]))
    staying, cross_0, cross_1 = to_columns(staying), to_y(crossing[:2]), to_y(crossing[2:])
    own, merged_keys = pl.pallas_call(
        compact_kernel,
        out_shape=[struct(ROWS, D), struct(128, 128)],
        in_specs=[VMEM] * NB,
        out_specs=[VMEM] * 2,
        compiler_params=params(12),
        cost_estimate=cost(2 * ROWS * NB * PAD * D, 2_700_000),
        name="compact",
    )(*msgs)

    back, front, p_own = along(own), against(own), to_y(own)
    staying, back, front, p_own, cross_0 = lax.optimization_barrier(
        (staying, back, front, p_own, cross_0)
    )
    staying_other, cross_0_other = to_core(staying), to_core(cross_0)
    p_own_a = p_own[:, :SPLIT_IN]
    far, p_back_a = along(back), along(p_own_a)
    cross_1, staying_other, cross_0_other, far, p_back_a = lax.optimization_barrier(
        (cross_1, staying_other, cross_0_other, far, p_back_a)
    )
    weights = [staying, staying_other, cross_0, cross_0_other, cross_1, to_core(cross_1)]
    weights += [w_down[0], down_other]
    p_far_a, p_front_a = along(p_back_a), against(p_own_a)
    p_back_b, p_far_b, p_front_b = (to_y(v[:, SPLIT_IN:]) for v in (back, far, front))
    far_a, far_b, back_a, back_b = feed_forward([(far,), (back,)], core, weights, "ffn_here_0")
    front_a, front_b, own_a, own_b = feed_forward(
        [(front,), (own,)], core, weights, "ffn_here_1"
    )
    p_far_a, p_front_a, p_back_b, p_far_b, far_a, front_a = lax.optimization_barrier(
        (p_far_a, p_front_a, p_back_b, p_far_b, far_a, front_a)
    )
    q_far_a, q_far_b, q_back_a, q_back_b = feed_forward(
        [(p_far_a, p_far_b), (p_back_a, p_back_b)], core, weights, "ffn_there_0"
    )
    got_0, passing = against(back_a), along(far_a)
    p_front_a, got_0, passing = lax.optimization_barrier((p_front_a, got_0, passing))
    q_front_a, q_front_b, q_own_a, q_own_b = feed_forward(
        [(p_front_a, p_front_b), (p_own,)], core, weights, "ffn_there_1"
    )
    got_1 = along(add(front_a, passing))
    got_2 = against(q_back_a)
    got_3 = along(add(q_front_a, along(q_far_a)))
    own_q = to_y(q_own_b)
    swapped = to_y((q_own_a.astype(F32) + got_2.astype(F32) + got_3.astype(F32)).astype(BF))
    got_5 = along(add(add(front_b, to_y(q_front_b)), along(add(far_b, to_y(q_far_b)))))
    got_4 = against(add(back_b, to_y(q_back_b)))

    sources = jnp.stack([(b // 2 - dz) % 4 * 2 + (b - dl) % 2 for dz, dl in REL_B])
    returns = pl.pallas_call(
        final_kernel,
        out_shape=struct(NB, BACK, D),
        in_specs=[SMEM] + [VMEM] * 8,
        out_specs=VMEM,
        compiler_params=params(16),
        cost_estimate=cost(2 * NB * BACK * ROWS * D, 6_000_000),
        name="spread",
    )(sources.astype(jnp.int32), own_a, got_0, got_1, swapped, own_b, own_q, got_4, got_5)
    results = lax.all_to_all(returns, "branch", 0, 0, tiled=True)
    mixed = pl.pallas_call(
        combine_kernel,
        out_shape=struct(TOK, D),
        in_specs=[VMEM] * 3,
        out_specs=VMEM,
        compiler_params=params(12),
        cost_estimate=cost(4 * NB * BACK * TOK * D, 2_200_000),
        name="combine",
    )(routes, gate_logits, results)
    return mixed, merged_keys


def solution(mesh):
    placed = (
        P(("branch", "fsdp"), None),
        P(("branch", "fsdp"), None),
        P(("branch", "fsdp"), None),
        P("branch", "fsdp", None),
        P("branch", "fsdp", None),
        P("branch", "fsdp", None),
        P("branch", "fsdp", None),
    )
    return jax.shard_map(
        per_device,
        mesh=mesh,
        in_specs=placed,
        out_specs=(P(("branch", "fsdp"), None), P("fsdp", "branch")),
        check_vma=False,
    )
```

```python
import functools

import jax
import jax.numpy as jnp
from jax import lax
from jax.experimental import pallas as pl
from jax.experimental.pallas import tpu as pltpu
from jax.sharding import PartitionSpec as P

BF = jnp.bfloat16
F32 = jnp.float32
NB = 8
CAP = 34
PAD = 48
BACK = 40
KEY_AT = 40
TOK = 128
D = 2048
SPLIT_IN = 1536
SPLIT_OUT = 1280
ROWS = NB * CAP
UNITS = 1024
REL_B = [(dz, dl) for dz in range(4) for dl in range(2)]
VMEM = pl.BlockSpec(memory_space=pltpu.VMEM)
HBM = pl.BlockSpec(memory_space=pltpu.HBM)
SMEM = pl.BlockSpec(memory_space=pltpu.SMEM)


def perm_f(dy, dx, dc):
    return [
        (y * 8 + x * 2 + c, (y + dy) % 2 * 8 + (x + dx) % 4 * 2 + (c + dc) % 2)
        for y in range(2)
        for x in range(4)
        for c in range(2)
    ]


RING = [
    (y * 8 + x * 2 + c, y * 8 + (x + 1 - 2 * c) % 4 * 2 + c)
    for y in range(2)
    for x in range(4)
    for c in range(2)
]


def perm_b(dz, dl):
    return [
        (z * 2 + w, (z + dz) % 4 * 2 + (w + dl) % 2) for z in range(4) for w in range(2)
    ]


def along(v):
    return lax.ppermute(v, "fsdp", RING)


def against(v):
    return lax.ppermute(v, "fsdp", [(d, s) for s, d in RING])


def to_y(v):
    return lax.ppermute(v, "fsdp", perm_f(1, 0, 0))


def to_columns(v):
    return lax.all_to_all(
        v, "fsdp", 0, 0, tiled=True,
        axis_index_groups=[[8 * y + 2 * k + c for k in range(4)] for y in range(2) for c in range(2)],
    )


def to_core(v):
    return lax.ppermute(v, "fsdp", perm_f(0, 0, 1))


def iota(shape, dim):
    return lax.broadcasted_iota(jnp.int32, shape, dim)


def positions(routes_ref):
    lane = iota((TOK, 128), 1)
    chosen = (routes_ref[:, 0:1] == lane) | (routes_ref[:, 1:2] == lane)
    earlier = (iota((TOK, TOK), 1) < iota((TOK, TOK), 0)).astype(F32).astype(BF)
    count = jnp.dot(earlier, chosen.astype(F32).astype(BF), preferred_element_type=F32)
    return jnp.where(chosen, count, -1.0)


def dispatch_kernel(experts, routes, tokens, keys, *outs):
    by_expert = positions(routes).T
    sub = iota((128, TOK), 0)
    for r, out in enumerate(outs):
        e = experts[r]
        place = jnp.sum(jnp.where(sub == e, by_expert, 0.0), axis=0, keepdims=True)
        pick = (place == iota((KEY_AT, TOK), 0).astype(F32)).astype(F32).astype(BF)
        rows = jnp.dot(pick, tokens[...], preferred_element_type=F32)
        key = keys[:, pl.ds(pl.multiple_of(e * 128, 128), 128)].astype(F32)
        strip = jnp.concatenate([key[8 * m : 8 * m + 8] for m in range(16)], axis=1)
        out[...] = jnp.concatenate([rows, strip], axis=0).astype(BF)


def slot_matrix(rows_dim, shape, pad):
    compact, padded = iota(shape, rows_dim), iota(shape, 1 - rows_dim)
    block = sum((padded >= pad * m).astype(jnp.int32) for m in range(1, NB))
    j = padded - pad * block
    return ((j < CAP) & (compact == block * CAP + j)).astype(F32).astype(BF)


def compact_kernel(*refs):
    msgs, (out, merged) = refs[:NB], refs[NB:]
    stacked = jnp.concatenate([m[...] for m in msgs], axis=0)
    pick = slot_matrix(0, (ROWS, NB * PAD), PAD)
    out[...] = jnp.dot(pick, stacked, preferred_element_type=F32).astype(BF)
    total = functools.reduce(lambda a, b: a + b, [m[...].astype(F32)[KEY_AT:] for m in msgs])
    key = jnp.concatenate([total[:, 128 * m : 128 * m + 128] for m in range(16)], axis=0)
    merged[...] = (key / NB).astype(BF)


def pack_kernel(first, gate, up, out):
    out[0, 0] = gate[...]
    out[0, 1] = up[...]


def pack(first, gate, up, name):
    return pl.pallas_call(
        pack_kernel,
        grid_spec=pltpu.PrefetchScalarGridSpec(
            num_scalar_prefetch=1,
            grid=(4,),
            in_specs=[pl.BlockSpec((128, UNITS), lambda j, first: (0, first[0] + j))] * 2,
            out_specs=pl.BlockSpec((1, 2, 128, UNITS), lambda j, first: (j, 0, 0, 0)),
        ),
        out_shape=struct(4, 2, 128, UNITS),
        compiler_params=params(60),
        cost_estimate=cost(0, 8_000_000),
        name="pack_" + name,
    )(first, gate, up)


def ffn_kernel(widths, core, *refs):
    nx = sum(len(w) for w in widths)
    xs, refs = refs[:nx], refs[nx:]
    sources, refs = refs[:8], refs[8:]
    outs, (hidden, held, down, sems) = refs[:4], refs[4:]
    c, y = core[0], core[1]
    every, low, high = pl.ds(0, 4), pl.ds(0, 2), pl.ds(2, 2)
    places = ((y, c, every), (y, 1 - c, every))
    places += ((1 - y, c, low), (1 - y, 1 - c, low), (1 - y, c, high), (1 - y, 1 - c, high))
    steps = []
    for n in range(4):
        cols = pl.ds(256 * n, 256)
        steps.append(
            [
                pltpu.make_async_copy(
                    src.at[:, :, :, cols], held.at[(*places[i], slice(None), slice(None), cols)],
                    sems.at[6 * n + i],
                )
                for i, src in enumerate(sources[:6])
            ]
        )
    steps.append(
        [
            pltpu.make_async_copy(src, down.at[places[i][1]], sems.at[24 + i])
            for i, src in enumerate(sources[6:])
        ]
    )
    for copy in steps[0] + steps[1]:
        copy.start()
    at, blocks = 0, []
    for block in widths:
        pieces = [xs[at + i][...] for i in range(len(block))]
        blocks.append(jnp.concatenate(pieces, axis=1) if len(pieces) > 1 else pieces[0])
        at += len(block)
    x = jnp.concatenate(blocks, axis=0)
    for n in range(4):
        for copy in steps[n]:
            copy.wait()
        if n < 3:
            for copy in steps[n + 2]:
                copy.start()
        cols = slice(256 * n, 256 * n + 256)
        weights = [
            jnp.concatenate([held[i // 4, j, i % 4, k, :, cols] for i in range(8) for j in range(2)])
            for k in range(2)
        ]
        g = jnp.dot(x, weights[0], preferred_element_type=F32)
        u = jnp.dot(x, weights[1], preferred_element_type=F32)
        hidden[:, cols] = (g * (1.0 / (1.0 + jnp.exp(-g))) * u).astype(BF)
    for copy in steps[4]:
        copy.wait()
    h = hidden[...]
    for at, end in ((0, SPLIT_OUT), (SPLIT_OUT, D)):
        for low in range(at, end, 512):
            high = min(low + 512, end)
            w = jnp.concatenate([down[j, :, low:high] for j in range(2)], axis=0)
            v = jnp.dot(h, w, preferred_element_type=F32).astype(BF)
            for i in range(2):
                outs[2 * i + (at > 0)][:, low - at : high - at] = v[i * ROWS : (i + 1) * ROWS]


def final_kernel(sources, *refs):
    parts, out = refs[:8], refs[8]
    total = []
    for k in range(2):
        addends = [p[...].astype(F32) for p in parts[4 * k : 4 * k + 4]]
        total.append(functools.reduce(lambda a, b: a + b, addends).astype(BF))
    rows = jnp.concatenate(total, axis=1)
    spread = slot_matrix(1, (NB * BACK, ROWS), BACK)
    wide = jnp.dot(spread, rows, preferred_element_type=F32)
    for r in range(NB):
        out[sources[r]] = wide[r * BACK : (r + 1) * BACK].astype(BF)


def combine_kernel(routes, logits, msgs, out):
    place = positions(routes)
    lane = iota((TOK, 128), 1)
    wide = iota((1, NB * BACK), 1)
    owner = sum((wide >= BACK * m).astype(jnp.int32) for m in range(1, NB))
    slot = (wide - BACK * owner).astype(F32)
    stacked = jnp.concatenate([msgs[r] for r in range(NB)], axis=0)
    gathered, score = [], []
    for k in range(2):
        route = routes[:, k : k + 1]
        mine = jnp.sum(jnp.where(lane == route, place, 0.0), axis=1, keepdims=True)
        pick = ((owner == route) & (slot == mine)).astype(F32).astype(BF)
        gathered.append(jnp.dot(pick, stacked, preferred_element_type=F32))
        lane8 = iota((TOK, NB), 1)
        score.append(jnp.sum(jnp.where(lane8 == route, logits[...], 0.0), axis=1, keepdims=True))
    diff = score[0] - score[1]
    w0 = 1.0 / (1.0 + jnp.exp(-diff))
    w1 = 1.0 / (1.0 + jnp.exp(diff))
    out[...] = (gathered[0] * w0 + gathered[1] * w1).astype(BF)


def cost(flops, nbytes, trans=0):
    return pl.CostEstimate(flops=flops, bytes_accessed=nbytes, transcendentals=trans)


def params(mib):
    return pltpu.CompilerParams(vmem_limit_bytes=mib * 2**20)


def struct(*shape):
    return jax.ShapeDtypeStruct(shape, BF)


def feed_forward(xs, core, weights, name):
    widths = tuple(tuple(v.shape[1] for v in block) for block in xs)
    flat = [v for block in xs for v in block]
    return pl.pallas_call(
        functools.partial(ffn_kernel, widths),
        out_shape=[struct(ROWS, SPLIT_OUT), struct(ROWS, D - SPLIT_OUT)] * 2,
        in_specs=[SMEM] + [VMEM] * len(flat) + [HBM] * 8,
        out_specs=[VMEM] * 4,
        scratch_shapes=[
            pltpu.VMEM((2 * ROWS, UNITS), BF),
            pltpu.VMEM((2, 2, 4, 2, 128, UNITS), BF),
            pltpu.VMEM((2, 512, D), BF),
            pltpu.SemaphoreType.DMA((26,)),
        ],
        compiler_params=params(46),
        cost_estimate=cost(6 * 2 * ROWS * D * UNITS, 18_000_000, 2 * ROWS * UNITS),
        name=name,
    )(core, *flat, *weights)


def add(a, b):
    return (a.astype(F32) + b.astype(F32)).astype(BF)


def per_device(tokens, routes, gate_logits, key_proj, w_gate, w_up, w_down):
    f = lax.axis_index("fsdp")
    y = f // 8
    core = jnp.stack([f % 2, y]).astype(jnp.int32)

    b = lax.axis_index("branch")
    experts = jnp.stack([(b // 2 + dz) % 4 * 2 + (b + dl) % 2 for dz, dl in REL_B])

    sends = pl.pallas_call(
        dispatch_kernel,
        out_shape=[struct(PAD, D)] * NB,
        grid=(1,),
        in_specs=[SMEM] + [pl.BlockSpec((TOK, n), lambda i: (0, 0)) for n in (2, D, 1024)],
        out_specs=[VMEM] * NB,
        compiler_params=params(12),
        cost_estimate=cost(2 * NB * PAD * TOK * D, 2_500_000),
        name="dispatch",
    )(experts.astype(jnp.int32), routes, tokens, key_proj[0])
    msgs = [sends[0]] + [
        lax.ppermute(sends[r], "branch", perm_b(*REL_B[r])) for r in range(1, NB)
    ]
    down_other = to_core(w_down[0])
    first = jnp.stack([4 * y, 4 - 4 * y]).astype(jnp.int32)
    crossing = pack(first[1:], w_gate[0], w_up[0], "other")
    crossing, down_other = lax.optimization_barrier((crossing, down_other))
    crossing = to_columns(crossing)
    staying = pack(first[:1], w_gate[0], w_up[0], "own")
    staying, crossing, msgs[1:6] = lax.optimization_barrier((staying, crossing, msgs[1:6]))
    staying, cross_0, cross_1 = to_columns(staying), to_y(crossing[:2]), to_y(crossing[2:])
    own, merged_keys = pl.pallas_call(
        compact_kernel,
        out_shape=[struct(ROWS, D), struct(128, 128)],
        in_specs=[VMEM] * NB,
        out_specs=[VMEM] * 2,
        compiler_params=params(12),
        cost_estimate=cost(2 * ROWS * NB * PAD * D, 2_700_000),
        name="compact",
    )(*msgs)

    back, front, p_own = along(own), against(own), to_y(own)
    staying, back, front, p_own, cross_0 = lax.optimization_barrier(
        (staying, back, front, p_own, cross_0)
    )
    staying_other, cross_0_other = to_core(staying), to_core(cross_0)
    p_own_a = p_own[:, :SPLIT_IN]
    far, p_back_a = along(back), along(p_own_a)
    cross_1, staying_other, cross_0_other, far, p_back_a = lax.optimization_barrier(
        (cross_1, staying_other, cross_0_other, far, p_back_a)
    )
    weights = [staying, staying_other, cross_0, cross_0_other, cross_1, to_core(cross_1)]
    weights += [w_down[0], down_other]
    p_far_a, p_front_a = along(p_back_a), against(p_own_a)
    p_back_b, p_far_b, p_front_b = (to_y(v[:, SPLIT_IN:]) for v in (back, far, front))
    far_a, far_b, back_a, back_b = feed_forward([(far,), (back,)], core, weights, "ffn_here_0")
    front_a, front_b, own_a, own_b = feed_forward(
        [(front,), (own,)], core, weights, "ffn_here_1"
    )
    p_far_a, p_front_a, p_back_b, p_far_b, far_a, front_a = lax.optimization_barrier(
        (p_far_a, p_front_a, p_back_b, p_far_b, far_a, front_a)
    )
    q_far_a, q_far_b, q_back_a, q_back_b = feed_forward(
        [(p_far_a, p_far_b), (p_back_a, p_back_b)], core, weights, "ffn_there_0"
    )
    got_0, passing = against(back_a), along(far_a)
    p_front_a, got_0, passing = lax.optimization_barrier((p_front_a, got_0, passing))
    q_front_a, q_front_b, q_own_a, q_own_b = feed_forward(
        [(p_front_a, p_front_b), (p_own,)], core, weights, "ffn_there_1"
    )
    got_1 = along(add(front_a, passing))
    got_2 = against(q_back_a)
    got_3 = along(add(q_front_a, along(q_far_a)))
    own_q = to_y(q_own_b)
    swapped = to_y((q_own_a.astype(F32) + got_2.astype(F32) + got_3.astype(F32)).astype(BF))
    got_5 = along(add(add(front_b, to_y(q_front_b)), along(add(far_b, to_y(q_far_b)))))
    got_4 = against(add(back_b, to_y(q_back_b)))

    sources = jnp.stack([(b // 2 - dz) % 4 * 2 + (b - dl) % 2 for dz, dl in REL_B])
    returns = pl.pallas_call(
        final_kernel,
        out_shape=struct(NB, BACK, D),
        in_specs=[SMEM] + [VMEM] * 8,
        out_specs=VMEM,
        compiler_params=params(16),
        cost_estimate=cost(2 * NB * BACK * ROWS * D, 6_000_000),
        name="spread",
    )(sources.astype(jnp.int32), own_a, got_0, got_1, swapped, own_b, own_q, got_4, got_5)
    results = lax.all_to_all(returns, "branch", 0, 0, tiled=True)
    mixed = pl.pallas_call(
        combine_kernel,
        out_shape=struct(TOK, D),
        in_specs=[VMEM] * 3,
        out_specs=VMEM,
        compiler_params=params(12),
        cost_estimate=cost(4 * NB * BACK * TOK * D, 2_200_000),
        name="combine",
    )(routes, gate_logits, results)
    return mixed, merged_keys


def solution(mesh):
    placed = (
        P(("branch", "fsdp"), None),
        P(("branch", "fsdp"), None),
        P(("branch", "fsdp"), None),
        P("branch", "fsdp", None),
        P("branch", "fsdp", None),
        P("branch", "fsdp", None),
        P("branch", "fsdp", None),
    )
    return jax.shard_map(
        per_device,
        mesh=mesh,
        in_specs=placed,
        out_specs=(P(("branch", "fsdp"), None), P("fsdp", "branch")),
        check_vma=False,
    )
```
